32 devices in a mesh: groups: 2 (over y), seq: 8 (over z, x), head: 1, sub: 2 (over core).
Axes of the slice: x: 2, y: 2, z: 4, core: 2. Of those that a mesh axis runs over, the one named last changes fastest.
Arguments:
- queries: bfloat16 [8, 32768, 512], P('head', ('groups', 'seq', 'sub')), parts along dimension 1, may hold values from -6 to 6
- keys: bfloat16 [8, 32768, 512], P('head', ('groups', 'seq', 'sub')), parts along dimension 1, may hold values from -6 to 6
- values: bfloat16 [8, 32768, 512], P('head', ('groups', 'seq', 'sub')), parts along dimension 1, may hold values from -6 to 6
- lr_codes: int32 [8, 32768], P('head', ('groups', 'seq', 'sub')), parts along dimension 1, may hold values from 0 to 15
- fast_gate: float32 [8, 512, 512], P('head', ('seq', 'sub')), may hold values from -0.25 to 0.25
- fast_up: float32 [8, 512, 512], P('head', ('seq', 'sub')), may hold values from -0.25 to 0.25
- fast_down: float32 [8, 512, 512], P('head', ('seq', 'sub')), may hold values from -0.25 to 0.25
Outputs:
- fast_out: bfloat16 [8, 32768, 512], P('head', ('groups', 'seq', 'sub')), parts along dimension 1
The draws below stay inside these ranges and needn't reach their ends.
There are 2 independent parts, one for each index of `groups`. The reference program is written for one: setup_inputs(seed, part) draws one part's arguments, and reference() takes and returns one part's arrays. A program takes and returns all parts, laid end to end along the dimension named above; an argument that names none is the same for every part. Nothing has to cross between parts.
All inputs are finite; a program needn't handle non-finite values.
Results may differ from the reference program's by a relative error of at most 0.0085.
Values may be sent and summed in bfloat16 or wider, within the bound.
A program may use at most 192 MiB of HBM per device.

```python
import jax
import jax.numpy as jnp
from jax import lax

HEADS = 8
FD = 512
FH = 512
BLOCK = 16384


def plant(entries, key, smallest, largest):
    longest = entries.shape.index(max(entries.shape))
    spots = []
    for shift in (0, 1):
        where = [jax.random.randint(jax.random.fold_in(key, axis), (), 0, length) for axis, length in enumerate(entries.shape)]
        where[longest] = (where[longest] + shift) % entries.shape[longest]
        spots.append(tuple(where))
    return entries.at[spots[0]].set(smallest).at[spots[1]].set(largest)


def raised(drawn, key, source, target, blocks, factor):
    owner, partner = [(jnp.arange(drawn.shape[dim]) // (drawn.shape[dim] // blocks)).reshape([-1 if axis == dim else 1 for axis in range(drawn.ndim)]) for dim in (source, target)]
    chosen = jax.random.permutation(key, blocks)[partner]
    strong = (owner == chosen) | (owner == (partner + blocks // 2) % blocks)
    return jnp.where(strong, factor * drawn, drawn)


def block_levels(stream_key, dims, cuts, smallest, top_value):
    def one(position, blocks):
        draws = jax.random.uniform(jax.random.fold_in(jax.random.fold_in(stream_key, 6), position), (blocks,), jnp.float32, smallest / len(cuts), top_value / len(cuts))
        return jnp.repeat(jnp.exp(draws), dims[position] // blocks).reshape((-1,) + (1,) * (len(dims) - position - 1))

    loudness = one(*cuts[0])
    for cut in cuts[1:]:
        loudness = loudness * one(*cut)
    return loudness


def scatter_about(stream_key, extent, scale, limit, pieces=(), kind=jnp.bfloat16):
    result = scale * jax.random.normal(stream_key, extent, jnp.float32)
    if pieces:
        result = result * block_levels(stream_key, extent, pieces, -0.22, 0.18)
    return jnp.clip(result, -limit, limit).astype(kind)


def bell_draw_with(rng, shape, width, limit, pieces, heavy, held_as=jnp.bfloat16):
    array = width * jax.random.normal(rng, shape, jnp.float32)
    if pieces:
        array = array * block_levels(rng, shape, pieces, -0.22, 0.18)
    return jnp.clip(raised(array, jax.random.fold_in(rng, 3), *heavy), -limit, limit).astype(held_as)


def setup_inputs(seed: int = 0, part: int = 0) -> dict:
    arg_keys = jax.random.split(jax.random.key(seed), 8)
    part_keys = jax.random.split(jax.random.fold_in(arg_keys[7], part), 8)
    return {
        "queries": scatter_about(part_keys[0], (HEADS, BLOCK, FD), 1.0, 6.0, ((1, 16),)),
        "keys": bell_draw_with(part_keys[1], (HEADS, BLOCK, FD), 1.0, 6.0, ((1, 16),), (1, 2, 16, 2.0)),
        "values": scatter_about(part_keys[2], (HEADS, BLOCK, FD), 1.0, 6.0, ((1, 16),)),
        "lr_codes": plant(jax.random.randint(part_keys[3], (HEADS, BLOCK), 0, 16), jax.random.fold_in(part_keys[3], 1), 0, 15).astype(jnp.int32),
        "fast_gate": scatter_about(arg_keys[4], (HEADS, FD, FH), FD ** -0.5, 0.25, ((1, 16),), jnp.float32),
        "fast_up": scatter_about(arg_keys[5], (HEADS, FD, FH), FD ** -0.5, 0.25, ((1, 16),), jnp.float32),
        "fast_down": scatter_about(arg_keys[6], (HEADS, FH, FD), FH ** -0.5, 0.25, ((1, 16),), jnp.float32),
    }


EPSILON = 1e-06
STEP_SIZE = 0.5

def renew(weight, grad):
    scale = STEP_SIZE * jnp.sqrt(jnp.sum(weight * weight) + EPSILON) / jnp.sqrt(jnp.sum(grad * grad) + EPSILON)
    moved = weight - scale * grad
    ratio = jnp.sqrt((lax.optimization_barrier(jnp.sum(weight * weight, axis=0)) + EPSILON) / (lax.optimization_barrier(jnp.sum(moved * moved, axis=0)) + EPSILON))
    return moved * ratio[None, :]

def one_head(operands):
    queries, keys, values, codes, gate_w, up_w, down_w = operands
    gate_b = gate_w.astype(jnp.bfloat16)
    up_b = up_w.astype(jnp.bfloat16)
    down_b = down_w.astype(jnp.bfloat16)
    gate_pre = jnp.dot(keys, gate_b, preferred_element_type=jnp.float32)
    up_pre = jnp.dot(keys, up_b, preferred_element_type=jnp.float32)
    sigmoid_gate = jax.nn.sigmoid(gate_pre)
    hidden = (gate_pre * sigmoid_gate * up_pre).astype(jnp.bfloat16)
    token_rates = (codes.astype(jnp.float32) + 1.0) / 16.0
    target = (-token_rates[:, None] * values.astype(jnp.float32)).astype(jnp.bfloat16)
    back = jnp.dot(target, down_b.T, preferred_element_type=jnp.float32)
    grad_gate_pre = (back * up_pre * sigmoid_gate * (1.0 + gate_pre * (1.0 - sigmoid_gate))).astype(jnp.bfloat16)
    grad_up_pre = (back * gate_pre * sigmoid_gate).astype(jnp.bfloat16)
    grad_gate = jnp.dot(keys.T, grad_gate_pre, preferred_element_type=jnp.float32)
    grad_up = jnp.dot(keys.T, grad_up_pre, preferred_element_type=jnp.float32)
    grad_down = jnp.dot(hidden.T, target, preferred_element_type=jnp.float32)
    new_gate = renew(gate_w, grad_gate).astype(jnp.bfloat16)
    new_up = renew(up_w, grad_up).astype(jnp.bfloat16)
    new_down = renew(down_w, grad_down).astype(jnp.bfloat16)
    query_gate = jnp.dot(queries, new_gate, preferred_element_type=jnp.float32)
    query_up = jnp.dot(queries, new_up, preferred_element_type=jnp.float32)
    query_hidden = (jax.nn.silu(query_gate) * query_up).astype(jnp.bfloat16)
    return jnp.dot(query_hidden, new_down, preferred_element_type=jnp.float32).astype(jnp.bfloat16)

def reference(queries, keys, values, lr_codes, fast_gate, fast_up, fast_down):
    return lax.map(one_head, (queries, keys, values, lr_codes, fast_gate, fast_up, fast_down))
```

```python
import functools

import jax
import jax.numpy as jnp
from jax import lax
from jax.experimental import pallas as pl
from jax.experimental.pallas import tpu as pltpu
from jax.sharding import PartitionSpec as P

EPSILON = 1e-06
STEP_SIZE = 0.5
WIDTH = 2
DEPTH = 4
VMEM_LIMIT = 54 * 1024 * 1024
BF = jnp.bfloat16
F32 = jnp.float32


def place_of(z):
    return jnp.where(2 * z < DEPTH, 2 * z, 2 * (DEPTH - 1 - z) + 1)


def device(z, x, s):
    return {"seq": z * WIDTH + x, "sub": s}


def greet(partners):
    barrier = pltpu.get_barrier_semaphore()
    for partner in partners:
        pl.semaphore_signal(barrier, inc=1, device_id=partner, device_id_type=pl.DeviceIdType.MESH)
    pl.semaphore_wait(barrier, len(partners))


def send(src, dst, send_sem, recv_sem, target):
    return pltpu.make_async_remote_copy(
        src_ref=src,
        dst_ref=dst,
        send_sem=send_sem,
        recv_sem=recv_sem,
        device_id=target,
        device_id_type=pl.DeviceIdType.MESH,
    )


def dot(a, b, dims=((1,), (0,))):
    return lax.dot_general(a, b, (dims, ((), ())), preferred_element_type=F32)


def owner(k):
    return jnp.where(k % 2 == 0, k // 2, DEPTH - 1 - k // 2)


def gather_units(rows):
    part = rows // 2
    return ((0, 0, rows, False), (1, 0, rows, False), (2, 0, part, False), (2, part, rows - part, True))


def step_kernel(
    gate_w, up_w, down_w, codes, keys, values, queries, out,
    full, stage, rates, tok, gsend, got_x, kept, zsum, got_z, new, norm_out, norm_in,
    ps, pr, cs, cr, ll, ls, lr, free,
    gs, gr, xs, xr, ys, yr,
    rxs, rxr, rzs, rzr, ns, nr,
    hsl, hsr, hr, fs, fr, os, orr,
):
    n = DEPTH
    z, x = lax.div(lax.axis_index("seq"), WIDTH), lax.rem(lax.axis_index("seq"), WIDTH)
    s, y = lax.axis_index("sub"), lax.axis_index("groups")
    feats = gate_w.shape[2]
    half = feats // 2
    mate, side = device(z, x, 1 - s), device(z, 1 - x, s)
    units = gather_units(feats)

    def cols(j):
        return pl.ds(pl.multiple_of(j * half, half), half)

    def here(src, g, i, k):
        return pltpu.make_async_copy(src.at[2 * k + s], tok.at[2 * lax.rem(g, 2) + i, s], ll.at[g, i])

    def there(src, g, i, k):
        return send(
            src.at[2 * k + 1 - s], tok.at[2 * lax.rem(g, 2) + i, s], ls.at[g, i], lr.at[g, i], mate
        )

    def load(g, what):
        def learning():
            what(keys, g, 0, g).start()
            what(values, g, 1, g).start()

        def applying():
            for i in range(2):
                what(queries, g, i, 2 * (g - n) + i).start()

        if isinstance(g, int):
            learning() if g < n else applying()
        else:
            pl.when(g < n)(learning)
            pl.when(g >= n)(applying)

    def loaded(g, i):
        here(keys, g, i, 0).wait()
        there(keys, g, i, 0).wait_recv()

    def pair(k):
        return send(stage.at[k], full.at[k, :, z, x, s], ps.at[k], pr.at[k], mate)

    def paired(k):
        block = full.at[k, :, z, x, 1 - s]
        return send(stage.at[k], block, ps.at[k], pr.at[k], mate)

    def along(k, zt):
        block = full.at[k, :, z, x, y]
        return send(block, block, gs.at[k, zt], gr.at[k, z], device(zt, x, s))

    def along_in(k, src):
        block = full.at[k, :, src, x, y]
        return send(block, block, gs.at[k, src], gr.at[k, src], device(src, x, s))

    def across(k, src, col):
        block = full.at[k, :, src, col, y]
        return send(block, block, xs.at[k, src], xr.at[k, src], side)

    def over(k, src, col, row):
        block = full.at[k, :, src, col, row]
        return send(block, block, ys.at[k, src, col], yr.at[k, src, col], {"groups": 1 - y})

    def others():
        return [lax.rem(z + d, n) for d in range(1, n)]

    def first(k):
        paired(k).wait_recv()
        for zt in others():
            along(k, zt).start()
        across(k, z, x).start()

    def second(k):
        for src in others():
            along_in(k, src).wait_recv()
            across(k, src, x).start()
            over(k, src, x, y).start()

    def third(k):
        for src in [z] + others():
            across(k, src, 1 - x).wait_recv()
            over(k, src, 1 - x, y).start()

    def swap(k, m):
        return send(gsend.at[k, m], got_x.at[k, m], rxs.at[k, m], rxr.at[k, m], side)

    def compute(k):
        for src in [z] + others():
            over(k, src, 1 - x, 1 - y).wait_recv()
        for src in others():
            over(k, src, x, 1 - y).wait_recv()
        for i in range(2):
            loaded(k, i)
        slot = 2 * lax.rem(k, 2)
        tokens = tok.shape[2]
        for c in range(2):
            rate = (rates[c, pl.ds(2 * k + s, 1), :].astype(F32) + 1.0) / 16.0
            rate = jnp.transpose(jnp.broadcast_to(rate, (128, tokens)))
            rate = jnp.concatenate([rate] * (feats // 128), axis=1)
            tok[slot + 1, c] = (-rate * tok[slot + 1, c].astype(F32)).astype(BF)
        for step, j in enumerate((1 - x, x)):
            gate = full[k, 0, :, :, :, :, cols(j)].reshape(feats, half)
            up = full[k, 1, :, :, :, :, cols(j)].reshape(feats, half)
            down = full[k, 2, pl.ds(j * (n // 2), n // 2)].reshape(half, feats)
            sums = [None] * 4
            for c in range(2):
                key, target = tok[slot, c], tok[slot + 1, c]
                gate_pre = dot(key, gate)
                up_pre = dot(key, up)
                back = dot(target, down, ((1,), (1,)))
                sig = jax.nn.sigmoid(gate_pre)
                silu = gate_pre * sig
                hidden = (silu * up_pre).astype(BF)
                ggp = (back * up_pre * sig * (1.0 + gate_pre * (1.0 - sig))).astype(BF)
                gup = (back * silu).astype(BF)
                terms = (
                    dot(key, ggp, ((0,), (0,))),
                    dot(key, gup, ((0,), (0,))),
                    dot(hidden, tok[slot + 1, c, :, cols(1 - x)], ((0,), (0,))),
                    dot(hidden, tok[slot + 1, c, :, cols(x)], ((0,), (0,))),
                )
                sums = [t if a is None else a + t for a, t in zip(sums, terms)]
            gsend[k, 2, cols(j), :] = sums[2].astype(BF)
            kept[k, 2, cols(j), :] = sums[3]
            for m in range(2):
                if step == 0:
                    gsend[k, m] = sums[m].astype(BF)
                    swap(k, m).start()
                else:
                    kept[k, m] = sums[m]
        swap(k, 2).start()
        pl.semaphore_signal(free, inc=1, device_id=mate, device_id_type=pl.DeviceIdType.MESH)
        load(k + 2, here)

    def refill(k):
        pl.semaphore_wait(free, 1)
        load(k + 2, there)

    def toward(k, m):
        return send(
            zsum.at[k, m], got_z.at[z, m], rzs.at[k, m], rzr.at[z, m], device(owner(k), x, s)
        )

    def summed(src, m):
        block = got_z.at[src, m]
        return send(block, block, rzs.at[0, m], rzr.at[src, m], device(src, x, s))

    def combine(k):
        for m in range(3):
            swap(k, m).wait_recv()

            @pl.when(z == owner(k))
            def _(m=m):
                kept[k, m] += got_x[k, m].astype(F32)

            @pl.when(z != owner(k))
            def _(m=m):
                zsum[k, m] = (kept[k, m] + got_x[k, m].astype(F32)).astype(BF)
                toward(k, m).start()

    def block(k, u, col):
        m, begin, count, _ = units[u]
        return new.at[k, col, m, pl.ds(begin, count)]

    def hop(k, u, c, onward):
        piece = block(k, u, 1 - x if c else x)
        sems = hsr if onward == 1 else hsl
        return send(piece, piece, sems.at[k, u, c], hr.at[k, u, c], device(z + onward, x, s))

    def share(k, u, out_col):
        piece = block(k, u, out_col)
        return send(piece, piece, fs.at[k, u], fr.at[k, u], side)

    def spread(k, u, c):
        pl.when(z > 0)(lambda: hop(k, u, c, -1).start())
        pl.when(z < n - 1)(lambda: hop(k, u, c, 1).start())

    def renew(k):
        def norms(m):
            return send(norm_out.at[m], norm_in.at[m], ns.at[m], nr.at[m], side)

        def own(m):
            return full[k, m, :, :, :, :, cols(x)].reshape(feats, half).astype(F32)

        weight_totals, col_weights = [], []
        for m in range(3):
            whole = full[k, m].reshape(feats, feats).astype(F32)
            weight_totals.append(jnp.sum(whole * whole, keepdims=True))
            col_weights.append(jnp.sum(own(m) * own(m), axis=0, keepdims=True))

        def gather(m):
            for src in others():
                summed(src, m).wait_recv()
                kept[k, m] += got_z[src, m].astype(F32)
            part = kept[k, m]
            norm_out[m] = jnp.broadcast_to(jnp.sum(part * part, keepdims=True), norm_out.shape[1:])
            norms(m).start()

        def move(m):
            norms(m).wait()
            grad_total = norm_out[m, :1, :1] + norm_in[m, :1, :1]
            scale = STEP_SIZE * jnp.sqrt(weight_totals[m] + EPSILON) / jnp.sqrt(grad_total + EPSILON)
            moved = own(m) - scale * kept[k, m]
            col_moved = jnp.sum(moved * moved, axis=0, keepdims=True)
            ratio = jnp.sqrt((col_weights[m] + EPSILON) / (col_moved + EPSILON))
            new[k, x, m] = (moved * ratio).astype(BF)
            for u in reversed(range(len(units))):
                if units[u][0] == m:
                    share(k, u, x).start()
                    if not units[u][3]:
                        spread(k, u, 0)

        gather(0)
        gather(1)
        move(0)
        gather(2)
        move(1)
        move(2)
        spread(k, 3, 0)
        share(k, 3, 1 - x).wait_recv()
        spread(k, 3, 1)

    def relay(d, u, c, early):
        for onward in (1, -1):
            src = z - d * onward
            end = (d == 1) & ((src == 0) | (src == n - 1))
            there = (src >= 0) & (src < n)

            @pl.when(there & (end if early else jnp.logical_not(end)))
            def _(src=src, onward=onward):
                k = place_of(src)
                hop(k, u, c, 0).wait_recv()

                @pl.when((z + onward >= 0) & (z + onward < n))
                def _():
                    hop(k, u, c, onward).start()

                if not units[u][3]:
                    share(k, u, x).start()

    def result(k, h):
        return send(tok.at[k, 1 - s], out.at[h], os.at[k], orr.at[k], mate)

    def apply(k):
        for u in range(3):
            share(k, u, 1 - x).wait_recv()
        for i in range(2):
            pl.when(lax.rem(k, 2) == i)(lambda i=i: loaded(n + k // 2, i))
        for step, c in enumerate((1 - s, s)):
            q = tok[k, c]
            total = [None, None]
            for j in range(2):
                gate = dot(q, new[k, j, 0])
                up = dot(q, new[k, j, 1])
                hidden = (gate * jax.nn.sigmoid(gate) * up).astype(BF)
                for i in range(2):
                    term = dot(hidden, new[k, i, 2, pl.ds(j * half, half), :])
                    total[i] = term if j == 0 else total[i] + term
            for i in range(2):
                if step == 0:
                    tok[k, 1 - s, :, pl.ds(i * half, half)] = total[i].astype(BF)
                else:
                    out[2 * k + s, :, pl.ds(i * half, half)] = total[i].astype(BF)
            if step == 0:
                result(k, 2 * k + s).start()

    for g in range(2):
        load(g, here)
    for k in range(n):
        for m, weight in enumerate((gate_w, up_w, down_w)):
            full[k, m, z, x, s] = weight[2 * k + s].astype(BF)
            stage[k, m] = weight[2 * k + 1 - s].astype(BF)
    rates[s] = codes[...]
    greet([device(zt, x, s) for zt in others()] + [side, mate, {"groups": 1 - y}])
    for k in range(n):
        pair(k).start()
    coded = send(codes, rates.at[s], cs, cr, mate)
    coded.start()
    for g in range(2):
        load(g, there)
    send(codes, rates.at[1 - s], cs, cr, mate).wait_recv()
    for k in range(n):
        first(k)

    def bring(k, carry):
        second(k)
        pl.when(k < n - 1)(lambda: third(k))
        return carry

    lax.fori_loop(0, n, bring, 0)

    def step(t, carry):
        def when(k, what):
            pl.when((k >= 0) & (k < n))(lambda: what(k))

        when(t, compute)
        pl.when(t == 0)(lambda: third(n - 1))
        when(t, refill)
        when(t - 1, combine)
        return carry

    lax.fori_loop(0, n + 1, step, 0)

    for u in range(len(units)):
        for c in range(2 if units[u][3] else 1):
            relay(1, u, c, True)
    renew(place_of(z))

    def outward(d, carry):
        @pl.when(d < n - 1)
        def _():
            for u in range(len(units)):
                for c in range(2 if units[u][3] else 1):
                    relay(d + 1, u, c, False)

        def at(i, carry):
            src = z + d * (1 - 2 * i)

            @pl.when((src >= 0) & (src < n) & ((d > 0) | (i == 0)))
            def _():
                apply(place_of(src))

            return carry

        return lax.fori_loop(0, 2, at, carry)

    lax.fori_loop(0, n, outward, 0)

    def last(k, carry):
        pair(k).wait_send()
        for zt in others():
            along(k, zt).wait_send()
        for src in [z] + others():
            across(k, src, x).wait_send()
            over(k, src, 1 - x, y).wait_send()
        for src in others():
            over(k, src, x, y).wait_send()
        for m in range(3):
            swap(k, m).wait_send()
            pl.when(z != owner(k))(lambda m=m: toward(k, m).wait_send())
        for u in range(len(units)):
            for c in range(2 if units[u][3] else 1):
                pl.when((z >= owner(k)) & (z < n - 1))(lambda u=u, c=c: hop(k, u, c, 1).wait_send())
                pl.when((z <= owner(k)) & (z > 0))(lambda u=u, c=c: hop(k, u, c, -1).wait_send())
            if not units[u][3]:
                share(k, u, x).wait_send()
            else:
                pl.when(z == owner(k))(lambda u=u: share(k, u, x).wait_send())
        result(k, 2 * k + 1 - s).wait()
        return carry

    lax.fori_loop(0, n, last, 0)
    for g in range(n + n // 2):
        for i in range(2):
            there(keys, g, i, 0).wait_send()
    coded.wait_send()


def whole_step(queries, keys, values, codes, gate_w, up_w, down_w):
    heads, rows, feats = gate_w.shape
    tokens = keys.shape[1]
    n = DEPTH
    half = feats // 2
    dma = pltpu.SemaphoreType.DMA
    vmem = pl.BlockSpec(memory_space=pltpu.VMEM)
    anywhere = pl.BlockSpec(memory_space=pl.ANY)
    piece = (3, feats, half)
    count = len(gather_units(feats))
    return pl.pallas_call(
        step_kernel,
        out_shape=pltpu.VMEM((heads, tokens, feats), BF),
        in_specs=[vmem] * 4 + [anywhere] * 3,
        out_specs=vmem,
        scratch_shapes=[
            pltpu.VMEM((n, 3, n, WIDTH, 2, rows, feats), BF),
            pltpu.VMEM((n, 3, rows, feats), BF),
            pltpu.VMEM((2, heads, tokens), jnp.int32),
            pltpu.VMEM((4, 2, tokens, feats), BF),
            pltpu.VMEM((n,) + piece, BF),
            pltpu.VMEM((n,) + piece, BF),
            pltpu.VMEM((n,) + piece, F32),
            pltpu.VMEM((n,) + piece, BF),
            pltpu.VMEM((n,) + piece, BF),
            pltpu.VMEM((n, 2) + piece, BF),
            pltpu.VMEM((3, 8, 128), F32),
            pltpu.VMEM((3, 8, 128), F32),
            dma((n,)), dma((n,)), dma(()), dma(()),
            *[dma((n + n // 2, 2))] * 3,
            pltpu.SemaphoreType.REGULAR,
            *[dma((n, n))] * 4,
            *[dma((n, n, WIDTH))] * 2,
            *[dma((n, 3))] * 4,
            *[dma((3,))] * 2,
            *[dma((n, count, 2))] * 3,
            *[dma((n, count))] * 2,
            *[dma((n,))] * 2,
        ],
        compiler_params=pltpu.CompilerParams(
            collective_id=0, has_side_effects=True, vmem_limit_bytes=VMEM_LIMIT
        ),
        name="whole_step",
    )(gate_w, up_w, down_w, codes, keys, values, queries)


def column_squares(matrix):
    return jnp.sum(matrix * matrix, axis=1)


def rescale(moved, col_weight, col_moved):
    return moved * jnp.sqrt((col_weight + EPSILON) / (col_moved + EPSILON))[:, None, :]


def step_scale(col_weight, grad_total):
    return (
        STEP_SIZE * jnp.sqrt(jnp.sum(col_weight, axis=1) + EPSILON) / jnp.sqrt(grad_total + EPSILON)
    )


def apply_rows(queries, gate_b, up_b, down_b):
    query_gate = jnp.einsum("htd,hdf->htf", queries, gate_b, preferred_element_type=jnp.float32)
    query_up = jnp.einsum("htd,hdf->htf", queries, up_b, preferred_element_type=jnp.float32)
    query_hidden = (jax.nn.silu(query_gate) * query_up).astype(jnp.bfloat16)
    return jnp.einsum(
        "htf,hfd->htd", query_hidden, down_b, preferred_element_type=jnp.float32
    ).astype(jnp.bfloat16)


def local_grads_rows(keys, target, gate_b, up_b, down_b):
    gate_pre = jnp.einsum("htd,hdf->htf", keys, gate_b, preferred_element_type=jnp.float32)
    up_pre = jnp.einsum("htd,hdf->htf", keys, up_b, preferred_element_type=jnp.float32)
    sigmoid_gate = jax.nn.sigmoid(gate_pre)
    hidden = (gate_pre * sigmoid_gate * up_pre).astype(jnp.bfloat16)
    back = jnp.einsum("htd,hfd->htf", target, down_b, preferred_element_type=jnp.float32)
    grad_gate_pre = (back * up_pre * sigmoid_gate * (1.0 + gate_pre * (1.0 - sigmoid_gate))).astype(
        jnp.bfloat16
    )
    grad_up_pre = (back * gate_pre * sigmoid_gate).astype(jnp.bfloat16)
    grad_gate = jnp.einsum("htd,htf->hdf", keys, grad_gate_pre, preferred_element_type=jnp.float32)
    grad_up = jnp.einsum("htd,htf->hdf", keys, grad_up_pre, preferred_element_type=jnp.float32)
    grad_down = jnp.einsum("htf,htd->hfd", hidden, target, preferred_element_type=jnp.float32)
    return (grad_gate, grad_up, grad_down)


def on_device_rows(queries, keys, values, lr_codes, fast_gate, fast_up, fast_down):
    token_rates = (lr_codes.astype(jnp.float32) + 1.0) / 16.0
    target = (-token_rates[:, :, None] * values.astype(jnp.float32)).astype(jnp.bfloat16)
    gate_b, up_b, down_b = (
        lax.all_gather(fast_gate.astype(jnp.bfloat16), ("seq", "sub"), axis=1, tiled=True),
        lax.all_gather(fast_up.astype(jnp.bfloat16), ("seq", "sub"), axis=1, tiled=True),
        lax.all_gather(fast_down.astype(jnp.bfloat16), ("seq", "sub"), axis=1, tiled=True),
    )
    grad_gate, grad_up, grad_down = local_grads_rows(keys, target, gate_b, up_b, down_b)
    owned = (
        lax.psum_scatter(grad_gate, ("seq", "sub"), scatter_dimension=1, tiled=True),
        lax.psum_scatter(grad_up, ("seq", "sub"), scatter_dimension=1, tiled=True),
        lax.psum_scatter(grad_down, ("seq", "sub"), scatter_dimension=1, tiled=True),
    )
    weights = (fast_gate, fast_up, fast_down)
    grad_local = jnp.stack(
        [
            jnp.sum(owned[0] * owned[0], axis=(1, 2)),
            jnp.sum(owned[1] * owned[1], axis=(1, 2)),
            jnp.sum(owned[2] * owned[2], axis=(1, 2)),
        ],
        axis=1,
    )
    col_gate, col_up, col_down, grad_totals = lax.psum(
        (column_squares(fast_gate), column_squares(fast_up), column_squares(fast_down), grad_local),
        ("seq", "sub"),
    )
    col_weights = (col_gate, col_up, col_down)
    moved_all = []
    for index in range(3):
        scale = step_scale(col_weights[index], grad_totals[:, index])
        moved_all.append(weights[index] - scale[:, None, None] * owned[index])
    moved_cols = lax.psum(
        (column_squares(moved_all[0]), column_squares(moved_all[1]), column_squares(moved_all[2])),
        ("seq", "sub"),
    )
    renewed = [
        rescale(moved_all[index], col_weights[index], moved_cols[index]).astype(jnp.bfloat16)
        for index in range(3)
    ]
    new_gate, new_up, new_down = (
        lax.all_gather(renewed[0], ("seq", "sub"), axis=1, tiled=True),
        lax.all_gather(renewed[1], ("seq", "sub"), axis=1, tiled=True),
        lax.all_gather(renewed[2], ("seq", "sub"), axis=1, tiled=True),
    )
    return apply_rows(queries, new_gate, new_up, new_down)


def solution(mesh):
    groups, seq, sub = (mesh.shape[axis] for axis in ("groups", "seq", "sub"))

    def on_device(*arrays):
        if groups == 2 and sub == 2 and seq == WIDTH * DEPTH and arrays[4].shape[0] == 2 * DEPTH:
            return whole_step(*arrays)
        return on_device_rows(*arrays)

    return jax.shard_map(
        on_device,
        mesh=mesh,
        in_specs=(
            P("head", ("groups", "seq", "sub"), None),
            P("head", ("groups", "seq", "sub"), None),
            P("head", ("groups", "seq", "sub"), None),
            P("head", ("groups", "seq", "sub")),
            P("head", ("seq", "sub"), None),
            P("head", ("seq", "sub"), None),
            P("head", ("seq", "sub"), None),
        ),
        out_specs=P("head", ("groups", "seq", "sub"), None),
        check_vma=False,
    )
```

```python
import functools

import jax
import jax.numpy as jnp
from jax import lax
from jax.experimental import pallas as pl
from jax.experimental.pallas import tpu as pltpu
from jax.sharding import PartitionSpec as P

EPSILON = 1e-06
STEP_SIZE = 0.5
WIDTH = 2
DEPTH = 4
VMEM_LIMIT = 54 * 1024 * 1024
BF = jnp.bfloat16
F32 = jnp.float32


def place_of(z):
    return jnp.where(2 * z < DEPTH, 2 * z, 2 * (DEPTH - 1 - z) + 1)


def device(z, x, s):
    return {"seq": z * WIDTH + x, "sub": s}


def greet(partners):
    barrier = pltpu.get_barrier_semaphore()
    for partner in partners:
        pl.semaphore_signal(barrier, inc=1, device_id=partner, device_id_type=pl.DeviceIdType.MESH)
    pl.semaphore_wait(barrier, len(partners))


def send(src, dst, send_sem, recv_sem, target):
    return pltpu.make_async_remote_copy(
        src_ref=src,
        dst_ref=dst,
        send_sem=send_sem,
        recv_sem=recv_sem,
        device_id=target,
        device_id_type=pl.DeviceIdType.MESH,
    )


def dot(a, b, dims=((1,), (0,))):
    return lax.dot_general(a, b, (dims, ((), ())), preferred_element_type=F32)


def owner(k):
    return jnp.where(k % 2 == 0, k // 2, DEPTH - 1 - k // 2)


def gather_units(rows):
    part = rows // 2
    return ((0, 0, rows, False), (1, 0, rows, False), (2, 0, part, False), (2, part, rows - part, True))


def step_kernel(
    gate_w, up_w, down_w, codes, keys, values, queries, out,
    full, stage, rates, tok, gsend, got_x, kept, zsum, got_m, got_z, new, norm_out, norm_in,
    ps, pr, cs, cr, ll, ls, lr, free,
    gs, gr, xs, xr, ys, yr,
    rxs, rxr, rzs, rmr, rzr, ns, nr,
    hsl, hsr, hr, fs, fr, os, orr,
):
    n = DEPTH
    z, x = lax.div(lax.axis_index("seq"), WIDTH), lax.rem(lax.axis_index("seq"), WIDTH)
    s, y = lax.axis_index("sub"), lax.axis_index("groups")
    feats = gate_w.shape[2]
    half = feats // 2
    mate, side = device(z, x, 1 - s), device(z, 1 - x, s)
    units = gather_units(feats)

    def cols(j):
        return pl.ds(pl.multiple_of(j * half, half), half)

    def here(src, g, i, k):
        return pltpu.make_async_copy(src.at[2 * k + s], tok.at[2 * lax.rem(g, 2) + i, s], ll.at[g, i])

    def there(src, g, i, k):
        return send(
            src.at[2 * k + 1 - s], tok.at[2 * lax.rem(g, 2) + i, s], ls.at[g, i], lr.at[g, i], mate
        )

    def load(g, what):
        def learning():
            what(keys, g, 0, g).start()
            what(values, g, 1, g).start()

        def applying():
            for i in range(2):
                what(queries, g, i, 2 * (g - n) + i).start()

        if isinstance(g, int):
            learning() if g < n else applying()
        else:
            pl.when(g < n)(learning)
            pl.when(g >= n)(applying)

    def loaded(g, i):
        here(keys, g, i, 0).wait()
        there(keys, g, i, 0).wait_recv()

    def pair(k):
        return send(stage.at[k], full.at[k, :, z, x, s], ps.at[k], pr.at[k], mate)

    def paired(k):
        block = full.at[k, :, z, x, 1 - s]
        return send(stage.at[k], block, ps.at[k], pr.at[k], mate)

    def along(k, zt):
        block = full.at[k, :, z, x, y]
        return send(block, block, gs.at[k, zt], gr.at[k, z], device(zt, x, s))

    def along_in(k, src):
        block = full.at[k, :, src, x, y]
        return send(block, block, gs.at[k, src], gr.at[k, src], device(src, x, s))

    def across(k, src, col):
        block = full.at[k, :, src, col, y]
        return send(block, block, xs.at[k, src], xr.at[k, src], side)

    def over(k, src, col, row):
        block = full.at[k, :, src, col, row]
        return send(block, block, ys.at[k, src, col], yr.at[k, src, col], {"groups": 1 - y})

    def others():
        return [lax.rem(z + d, n) for d in range(1, n)]

    def first(k):
        paired(k).wait_recv()
        for zt in others():
            along(k, zt).start()
        across(k, z, x).start()

    def second(k):
        for src in others():
            along_in(k, src).wait_recv()
            across(k, src, x).start()
            over(k, src, x, y).start()

    def third(k):
        for src in [z] + others():
            across(k, src, 1 - x).wait_recv()
            over(k, src, 1 - x, y).start()

    def swap(k, m):
        return send(gsend.at[k, m], got_x.at[k, m], rxs.at[k, m], rxr.at[k, m], side)

    def compute(k):
        for src in [z] + others():
            over(k, src, 1 - x, 1 - y).wait_recv()
        for src in others():
            over(k, src, x, 1 - y).wait_recv()
        for i in range(2):
            loaded(k, i)
        slot = 2 * lax.rem(k, 2)
        tokens = tok.shape[2]
        for c in range(2):
            rate = (rates[c, pl.ds(2 * k + s, 1), :].astype(F32) + 1.0) / 16.0
            rate = jnp.transpose(jnp.broadcast_to(rate, (128, tokens)))
            rate = jnp.concatenate([rate] * (feats // 128), axis=1)
            tok[slot + 1, c] = (-rate * tok[slot + 1, c].astype(F32)).astype(BF)
        for step, j in enumerate((1 - x, x)):
            gate = full[k, 0, :, :, :, :, cols(j)].reshape(feats, half)
            up = full[k, 1, :, :, :, :, cols(j)].reshape(feats, half)
            down = full[k, 2, pl.ds(j * (n // 2), n // 2)].reshape(half, feats)
            sums = [None] * 4
            for c in range(2):
                key, target = tok[slot, c], tok[slot + 1, c]
                gate_pre = dot(key, gate)
                up_pre = dot(key, up)
                back = dot(target, down, ((1,), (1,)))
                sig = jax.nn.sigmoid(gate_pre)
                silu = gate_pre * sig
                hidden = (silu * up_pre).astype(BF)
                ggp = (back * up_pre * sig * (1.0 + gate_pre * (1.0 - sig))).astype(BF)
                gup = (back * silu).astype(BF)
                terms = (
                    dot(key, ggp, ((0,), (0,))),
                    dot(key, gup, ((0,), (0,))),
                    dot(hidden, tok[slot + 1, c, :, cols(1 - x)], ((0,), (0,))),
                    dot(hidden, tok[slot + 1, c, :, cols(x)], ((0,), (0,))),
                )
                sums = [t if a is None else a + t for a, t in zip(sums, terms)]
            gsend[k, 2, cols(j), :] = sums[2].astype(BF)
            kept[k, 2, cols(j), :] = sums[3]
            for m in range(2):
                if step == 0:
                    gsend[k, m] = sums[m].astype(BF)
                    swap(k, m).start()
                else:
                    kept[k, m] = sums[m]
        descend(k)
        pl.semaphore_signal(free, inc=1, device_id=mate, device_id_type=pl.DeviceIdType.MESH)
        load(k + 2, here)

    def refill(k):
        pl.semaphore_wait(free, 1)
        load(k + 2, there)

    def far(k):
        return jnp.where(2 * owner(k) < n, n - 1, 0)

    def middle(k):
        return jnp.where(2 * owner(k) < n, n - 2, 1)

    def leaving(k, m):
        return zsum.at[k, m] if m < 3 else gsend.at[k, 2]

    def inward(k, m):
        return send(
            leaving(k, m), got_m.at[k // 2, m], rzs.at[k, m], rmr.at[k // 2, m], device(middle(k), x, s)
        )

    def toward(k, m, slot):
        return send(
            leaving(k, m), got_z.at[slot, m], rzs.at[k, m], rzr.at[slot, m], device(owner(k), x, s)
        )

    def leave(k, m):
        pl.when(z == far(k))(lambda: inward(k, m).start())
        pl.when(z != far(k))(lambda: toward(k, m, 1).start())

    def descend(k):
        @pl.when((z != owner(k)) & (z != middle(k)))
        def _():
            zsum[k, 2] = kept[k, 2].astype(BF)
            leave(k, 2)
            leave(k, 3)

    def combine(k):
        for m in range(2):
            swap(k, m).wait_recv()

            @pl.when((z == owner(k)) | (z == middle(k)))
            def _(m=m):
                kept[k, m] += got_x[k, m].astype(F32)

            @pl.when((z != owner(k)) & (z != middle(k)))
            def _(m=m):
                zsum[k, m] = (kept[k, m] + got_x[k, m].astype(F32)).astype(BF)
                leave(k, m)

    def bridge(k):
        @pl.when(z == middle(k))
        def _():
            for m in (2, 3, 0, 1):
                inward(k, m).wait_recv()
                if m < 3:
                    zsum[k, m] = (kept[k, m] + got_m[k // 2, m].astype(F32)).astype(BF)
                else:
                    gsend[k, 2] = (gsend[k, 2].astype(F32) + got_m[k // 2, m].astype(F32)).astype(BF)
                toward(k, m, 0).start()

    def block(k, u, col):
        m, begin, count, _ = units[u]
        return new.at[k, col, m, pl.ds(begin, count)]

    def hop(k, u, c, onward):
        piece = block(k, u, 1 - x if c else x)
        sems = hsr if onward == 1 else hsl
        return send(piece, piece, sems.at[k, u, c], hr.at[k, u, c], device(z + onward, x, s))

    def share(k, u, out_col):
        piece = block(k, u, out_col)
        return send(piece, piece, fs.at[k, u], fr.at[k, u], side)

    def spread(k, u, c):
        pl.when(z > 0)(lambda: hop(k, u, c, -1).start())
        pl.when(z < n - 1)(lambda: hop(k, u, c, 1).start())

    def renew(k):
        def norms(m):
            return send(norm_out.at[m], norm_in.at[m], ns.at[m], nr.at[m], side)

        def own(m):
            return full[k, m, :, :, :, :, cols(x)].reshape(feats, half).astype(F32)

        weight_totals, col_weights = [], []
        for m in range(3):
            whole = full[k, m].reshape(feats, feats).astype(F32)
            weight_totals.append(jnp.sum(whole * whole, keepdims=True))
            col_weights.append(jnp.sum(own(m) * own(m), axis=0, keepdims=True))

        def gather(m):
            for slot in range(2):
                toward(k, m, slot).wait_recv()
                kept[k, m] += got_z[slot, m].astype(F32)

        def measure(m):
            part = kept[k, m]
            norm_out[m] = jnp.broadcast_to(jnp.sum(part * part, keepdims=True), norm_out.shape[1:])
            norms(m).start()

        def move(m):
            norms(m).wait()
            grad_total = norm_out[m, :1, :1] + norm_in[m, :1, :1]
            scale = STEP_SIZE * jnp.sqrt(weight_totals[m] + EPSILON) / jnp.sqrt(grad_total + EPSILON)
            moved = own(m) - scale * kept[k, m]
            col_moved = jnp.sum(moved * moved, axis=0, keepdims=True)
            ratio = jnp.sqrt((col_weights[m] + EPSILON) / (col_moved + EPSILON))
            new[k, x, m] = (moved * ratio).astype(BF)
            for u in range(len(units)):
                if units[u][0] == m:
                    if not units[u][3]:
                        spread(k, u, 0)
            for u in reversed(range(len(units))):
                if units[u][0] == m:
                    share(k, u, x).start()

        for slot in range(2):
            toward(k, 3, slot).wait_recv()
        both = got_z[0, 3].astype(F32) + got_z[1, 3].astype(F32)
        gsend[k, 2] = (gsend[k, 2].astype(F32) + both).astype(BF)
        swap(k, 2).start()
        gather(0)
        measure(0)
        gather(2)
        move(0)
        gather(1)
        measure(1)
        swap(k, 2).wait_recv()
        kept[k, 2] += got_x[k, 2].astype(F32)
        measure(2)
        move(1)
        move(2)
        spread(k, 3, 0)
        share(k, 3, 1 - x).wait_recv()
        spread(k, 3, 1)

    def relay(d, u, c):
        for onward in (1, -1):
            src = z - d * onward

            @pl.when((src >= 0) & (src < n))
            def _(src=src, onward=onward):
                k = place_of(src)
                hop(k, u, c, 0).wait_recv()

                @pl.when((z + onward >= 0) & (z + onward < n))
                def _():
                    hop(k, u, c, onward).start()

                if not units[u][3]:
                    share(k, u, x).start()

    def result(k, h):
        return send(tok.at[k, 1 - s], out.at[h], os.at[k], orr.at[k], mate)

    def apply(k):
        for u in range(len(units) - 1):
            share(k, u, 1 - x).wait_recv()
        for i in range(2):
            pl.when(lax.rem(k, 2) == i)(lambda i=i: loaded(n + k // 2, i))
        for step, c in enumerate((1 - s, s)):
            q = tok[k, c]
            total = [None, None]
            for j in range(2):
                gate = dot(q, new[k, j, 0])
                up = dot(q, new[k, j, 1])
                hidden = (gate * jax.nn.sigmoid(gate) * up).astype(BF)
                for i in range(2):
                    term = dot(hidden, new[k, i, 2, pl.ds(j * half, half), :])
                    total[i] = term if j == 0 else total[i] + term
            for i in range(2):
                if step == 0:
                    tok[k, 1 - s, :, pl.ds(i * half, half)] = total[i].astype(BF)
                else:
                    out[2 * k + s, :, pl.ds(i * half, half)] = total[i].astype(BF)
            if step == 0:
                result(k, 2 * k + s).start()

    for g in range(2):
        load(g, here)
    for k in range(n):
        for m, weight in enumerate((gate_w, up_w, down_w)):
            full[k, m, z, x, s] = weight[2 * k + s].astype(BF)
            stage[k, m] = weight[2 * k + 1 - s].astype(BF)
    rates[s] = codes[...]
    greet([device(zt, x, s) for zt in others()] + [side, mate, {"groups": 1 - y}])
    for k in range(n):
        pair(k).start()
    coded = send(codes, rates.at[s], cs, cr, mate)
    coded.start()
    for g in range(2):
        load(g, there)
    send(codes, rates.at[1 - s], cs, cr, mate).wait_recv()
    for k in range(n):
        first(k)

    def bring(k, carry):
        second(k)
        pl.when(k < n - 1)(lambda: third(k))
        return carry

    lax.fori_loop(0, n, bring, 0)

    def step(t, carry):
        def when(k, what):
            pl.when((k >= 0) & (k < n))(lambda: what(k))

        when(t, compute)
        pl.when(t == 0)(lambda: third(n - 1))
        when(t, refill)
        when(t - 2, bridge)
        when(t - 1, combine)
        return carry

    lax.fori_loop(0, n + 2, step, 0)

    pieces = ((0, 0), (1, 0), (2, 0), (3, 0), (3, 1))
    renew(place_of(z))

    def outward(d, carry):
        @pl.when(d < n - 1)
        def _():
            for u, c in pieces[:-1]:
                relay(d + 1, u, c)

        pl.when(d < n - 2)(lambda: relay(d + 1, *pieces[-1]))

        def at(i, carry):
            src = z + d * (1 - 2 * i)
            there = (src >= 0) & (src < n) & ((d > 0) | (i == 0))
            pl.when(there)(lambda: apply(place_of(src)))
            return carry

        lax.fori_loop(0, 2, at, carry)

        pl.when(d == n - 2)(lambda: relay(d + 1, *pieces[-1]))
        return carry

    lax.fori_loop(0, n, outward, 0)

    def last(k, carry):
        pair(k).wait_send()
        for zt in others():
            along(k, zt).wait_send()
        for src in [z] + others():
            across(k, src, x).wait_send()
            over(k, src, 1 - x, y).wait_send()
        for src in others():
            over(k, src, x, y).wait_send()
        for m in range(2):
            swap(k, m).wait_send()
        pl.when(z == owner(k))(lambda: swap(k, 2).wait_send())
        for m in range(4):
            pl.when(z != owner(k))(lambda m=m: toward(k, m, 0).wait_send())
        for u in range(len(units)):
            for c in range(2 if units[u][3] else 1):
                pl.when((z >= owner(k)) & (z < n - 1))(lambda u=u, c=c: hop(k, u, c, 1).wait_send())
                pl.when((z <= owner(k)) & (z > 0))(lambda u=u, c=c: hop(k, u, c, -1).wait_send())
            if not units[u][3]:
                share(k, u, x).wait_send()
            else:
                pl.when(z == owner(k))(lambda u=u: share(k, u, x).wait_send())
        result(k, 2 * k + 1 - s).wait()
        return carry

    lax.fori_loop(0, n, last, 0)
    for g in range(n + n // 2):
        for i in range(2):
            there(keys, g, i, 0).wait_send()
    coded.wait_send()


def whole_step(queries, keys, values, codes, gate_w, up_w, down_w):
    heads, rows, feats = gate_w.shape
    tokens = keys.shape[1]
    n = DEPTH
    half = feats // 2
    dma = pltpu.SemaphoreType.DMA
    vmem = pl.BlockSpec(memory_space=pltpu.VMEM)
    anywhere = pl.BlockSpec(memory_space=pl.ANY)
    piece = (3, feats, half)
    count = len(gather_units(feats))
    return pl.pallas_call(
        step_kernel,
        out_shape=pltpu.VMEM((heads, tokens, feats), BF),
        in_specs=[vmem] * 4 + [anywhere] * 3,
        out_specs=vmem,
        scratch_shapes=[
            pltpu.VMEM((n, 3, n, WIDTH, 2, rows, feats), BF),
            pltpu.VMEM((n, 3, rows, feats), BF),
            pltpu.VMEM((2, heads, tokens), jnp.int32),
            pltpu.VMEM((4, 2, tokens, feats), BF),
            pltpu.VMEM((n,) + piece, BF),
            pltpu.VMEM((n,) + piece, BF),
            pltpu.VMEM((n,) + piece, F32),
            pltpu.VMEM((n,) + piece, BF),
            pltpu.VMEM((2, 4, feats, half), BF),
            pltpu.VMEM((2, 4, feats, half), BF),
            pltpu.VMEM((n, 2) + piece, BF),
            pltpu.VMEM((3, 8, 128), F32),
            pltpu.VMEM((3, 8, 128), F32),
            dma((n,)), dma((n,)), dma(()), dma(()),
            *[dma((n + n // 2, 2))] * 3,
            pltpu.SemaphoreType.REGULAR,
            *[dma((n, n))] * 4,
            *[dma((n, n, WIDTH))] * 2,
            *[dma((n, 3))] * 2,
            dma((n, 4)),
            *[dma((2, 4))] * 2,
            *[dma((3,))] * 2,
            *[dma((n, count, 2))] * 3,
            *[dma((n, count))] * 2,
            *[dma((n,))] * 2,
        ],
        compiler_params=pltpu.CompilerParams(
            collective_id=0, has_side_effects=True, vmem_limit_bytes=VMEM_LIMIT
        ),
        name="whole_step",
    )(gate_w, up_w, down_w, codes, keys, values, queries)


def column_squares(matrix):
    return jnp.sum(matrix * matrix, axis=1)


def rescale(moved, col_weight, col_moved):
    return moved * jnp.sqrt((col_weight + EPSILON) / (col_moved + EPSILON))[:, None, :]


def step_scale(col_weight, grad_total):
    return (
        STEP_SIZE * jnp.sqrt(jnp.sum(col_weight, axis=1) + EPSILON) / jnp.sqrt(grad_total + EPSILON)
    )


def apply_rows(queries, gate_b, up_b, down_b):
    query_gate = jnp.einsum("htd,hdf->htf", queries, gate_b, preferred_element_type=jnp.float32)
    query_up = jnp.einsum("htd,hdf->htf", queries, up_b, preferred_element_type=jnp.float32)
    query_hidden = (jax.nn.silu(query_gate) * query_up).astype(jnp.bfloat16)
    return jnp.einsum(
        "htf,hfd->htd", query_hidden, down_b, preferred_element_type=jnp.float32
    ).astype(jnp.bfloat16)


def local_grads_rows(keys, target, gate_b, up_b, down_b):
    gate_pre = jnp.einsum("htd,hdf->htf", keys, gate_b, preferred_element_type=jnp.float32)
    up_pre = jnp.einsum("htd,hdf->htf", keys, up_b, preferred_element_type=jnp.float32)
    sigmoid_gate = jax.nn.sigmoid(gate_pre)
    hidden = (gate_pre * sigmoid_gate * up_pre).astype(jnp.bfloat16)
    back = jnp.einsum("htd,hfd->htf", target, down_b, preferred_element_type=jnp.float32)
    grad_gate_pre = (back * up_pre * sigmoid_gate * (1.0 + gate_pre * (1.0 - sigmoid_gate))).astype(
        jnp.bfloat16
    )
    grad_up_pre = (back * gate_pre * sigmoid_gate).astype(jnp.bfloat16)
    grad_gate = jnp.einsum("htd,htf->hdf", keys, grad_gate_pre, preferred_element_type=jnp.float32)
    grad_up = jnp.einsum("htd,htf->hdf", keys, grad_up_pre, preferred_element_type=jnp.float32)
    grad_down = jnp.einsum("htf,htd->hfd", hidden, target, preferred_element_type=jnp.float32)
    return (grad_gate, grad_up, grad_down)


def on_device_rows(queries, keys, values, lr_codes, fast_gate, fast_up, fast_down):
    token_rates = (lr_codes.astype(jnp.float32) + 1.0) / 16.0
    target = (-token_rates[:, :, None] * values.astype(jnp.float32)).astype(jnp.bfloat16)
    gate_b, up_b, down_b = (
        lax.all_gather(fast_gate.astype(jnp.bfloat16), ("seq", "sub"), axis=1, tiled=True),
        lax.all_gather(fast_up.astype(jnp.bfloat16), ("seq", "sub"), axis=1, tiled=True),
        lax.all_gather(fast_down.astype(jnp.bfloat16), ("seq", "sub"), axis=1, tiled=True),
    )
    grad_gate, grad_up, grad_down = local_grads_rows(keys, target, gate_b, up_b, down_b)
    owned = (
        lax.psum_scatter(grad_gate, ("seq", "sub"), scatter_dimension=1, tiled=True),
        lax.psum_scatter(grad_up, ("seq", "sub"), scatter_dimension=1, tiled=True),
        lax.psum_scatter(grad_down, ("seq", "sub"), scatter_dimension=1, tiled=True),
    )
    weights = (fast_gate, fast_up, fast_down)
    grad_local = jnp.stack(
        [
            jnp.sum(owned[0] * owned[0], axis=(1, 2)),
            jnp.sum(owned[1] * owned[1], axis=(1, 2)),
            jnp.sum(owned[2] * owned[2], axis=(1, 2)),
        ],
        axis=1,
    )
    col_gate, col_up, col_down, grad_totals = lax.psum(
        (column_squares(fast_gate), column_squares(fast_up), column_squares(fast_down), grad_local),
        ("seq", "sub"),
    )
    col_weights = (col_gate, col_up, col_down)
    moved_all = []
    for index in range(3):
        scale = step_scale(col_weights[index], grad_totals[:, index])
        moved_all.append(weights[index] - scale[:, None, None] * owned[index])
    moved_cols = lax.psum(
        (column_squares(moved_all[0]), column_squares(moved_all[1]), column_squares(moved_all[2])),
        ("seq", "sub"),
    )
    renewed = [
        rescale(moved_all[index], col_weights[index], moved_cols[index]).astype(jnp.bfloat16)
        for index in range(3)
    ]
    new_gate, new_up, new_down = (
        lax.all_gather(renewed[0], ("seq", "sub"), axis=1, tiled=True),
        lax.all_gather(renewed[1], ("seq", "sub"), axis=1, tiled=True),
        lax.all_gather(renewed[2], ("seq", "sub"), axis=1, tiled=True),
    )
    return apply_rows(queries, new_gate, new_up, new_down)


def solution(mesh):
    groups, seq, sub = (mesh.shape[axis] for axis in ("groups", "seq", "sub"))

    def on_device(*arrays):
        if groups == 2 and sub == 2 and seq == WIDTH * DEPTH and arrays[4].shape[0] == 2 * DEPTH:
            return whole_step(*arrays)
        return on_device_rows(*arrays)

    return jax.shard_map(
        on_device,
        mesh=mesh,
        in_specs=(
            P("head", ("groups", "seq", "sub"), None),
            P("head", ("groups", "seq", "sub"), None),
            P("head", ("groups", "seq", "sub"), None),
            P("head", ("groups", "seq", "sub")),
            P("head", ("seq", "sub"), None),
            P("head", ("seq", "sub"), None),
            P("head", ("seq", "sub"), None),
        ),
        out_specs=P("head", ("groups", "seq", "sub"), None),
        check_vma=False,
    )
```
